32 devices in a mesh: groups: 2 (over x), fsdp: 16 (over z, y, core).
Axes of the slice: x: 2, y: 2, z: 4, core: 2. Of those that a mesh axis runs over, the one named last changes fastest.
Arguments:
- qkv: bfloat16 [8192, 9600], P(('groups', 'fsdp')), parts along dimension 0, may hold values from -22.5 to 22.5
- patches: bfloat16 [8192, 3200], P(('groups', 'fsdp')), parts along dimension 0, may hold values from -40 to 40
- frame_starts: int32 [2048], P(('groups', 'fsdp')), parts along dimension 0, may hold values from 0 to 1, as said below
- out_weight: bfloat16 [3200, 3200], P(None, 'fsdp'), may hold values from -0.109375 to 0.109375
- layer_scale: float32 [3200], replicated, may hold values from 0.5 to 5
- norm_gain: float32 [12800], replicated, may hold values from 0.1 to 1.9
- norm_bias: float32 [12800], replicated, may hold values from -3 to 3
- owners: int32 [2048, 1], P(('groups', 'fsdp')), parts along dimension 0, may hold values from 0 to 15; in each aligned block of 64 rows (0 to 63, 64 to 127, ...) at most 8 rows name the same one
Outputs:
- owned: bfloat16 [4096, 12800], P(('groups', 'fsdp')), parts along dimension 0
The draws below stay inside these ranges and needn't reach their ends.
There are 2 independent parts, one for each index of `groups`. The reference program is written for one: setup_inputs(seed, part) draws one part's arguments, and reference() takes and returns one part's arrays. A program takes and returns all parts, laid end to end along the dimension named above; an argument that names none is the same for every part. Nothing has to cross between parts.
Inputs may be any that keep to these rules, and one draw needn't show every extreme that they name: `frame_starts`: 1 at the first merged row of each device's block of 64, so frames never cross a block. `owners`: in each aligned block of 64 merged rows (one device's) no owner is named more than 8 times.
All inputs are finite; a program needn't handle non-finite values.
Results may differ from the reference program's by a relative error of at most 0.0095.
Values may be sent and summed in bfloat16 or wider, within the bound.
A program may use at most 128 MiB of HBM per device.

```python
import math
import jax
import jax.numpy as jnp
import numpy as np
from jax import lax

D = 3200
HEADS = 25
HEAD_DIM = 128
TOK_DEV = 256
QUAD_DEV = 64
TOKENS = 4096
QUADS = 1024
CAP = 8
SLOTS = 128
N_FSDP = 16


def draw_qkv(key, part):
    key = jax.random.fold_in(key, 11)
    first_key = jax.random.fold_in(key, 0)
    base = jnp.clip(jax.random.normal(first_key, (TOKENS, 3 * D), jnp.float32), -6.0, 6.0)
    return base.astype(jnp.bfloat16)


def draw_patches(key, part):
    key = jax.random.fold_in(key, 7)
    first_key, second_key = jax.random.split(key)
    row_scale = jnp.exp(jax.random.uniform(second_key, (TOKENS, 1), jnp.float32, 0.0, 2.302585))
    base = jnp.clip(jax.random.normal(first_key, (TOKENS, D), jnp.float32), -4.0, 4.0)
    return (base * row_scale).astype(jnp.bfloat16)


def draw_frame_starts(key, part):
    key = jax.random.fold_in(key, 5)
    picks = jax.random.randint(key, (QUADS,), 0, 8)
    starts = (picks == 0).astype(jnp.int32)
    leading = jnp.arange(QUADS) % QUAD_DEV == 0
    return jnp.where(leading, 1, starts).astype(jnp.int32)


def block_scale(key, dims, cuts, least, largest):
    def one(dim, parts):
        draws = jax.random.uniform(jax.random.fold_in(jax.random.fold_in(key, 6), dim), (parts,), jnp.float32, least / len(cuts), largest / len(cuts))
        return jnp.repeat(jnp.exp(draws), dims[dim] // parts).reshape((-1,) + (1,) * (len(dims) - dim - 1))

    factor_of = one(*cuts[0])
    for cut in cuts[1:]:
        factor_of = factor_of * one(*cut)
    return factor_of


def deal_out(key, own, number, rows, count, top, most, skew):
    order = jax.random.permutation(key, count)
    heavy_load, usual = portions_of(count, rows * top, most, skew, True), portions_of(count, rows * top, most, skew, False)
    places = jnp.arange(count)

    def named(sizes, turn):
        used = int((sizes > 0).sum())
        fixed = max(1, used // 4)
        moved = fixed + (places - fixed + turn * (used - fixed)) % max(1, count - fixed)
        return jnp.zeros((count,), jnp.int32).at[order[jnp.where(places < fixed, places, moved)]].set(jnp.asarray(sizes, jnp.int32))

    sizes = jnp.where(number % 4 == 0, named(heavy_load, number // 4), named(usual, number - number // 4 - 1))
    mixed = jax.random.permutation(jax.random.fold_in(own, 3), count)
    source_of, taker = mixed[0:count // 2 * 2:2], mixed[1:count // 2 * 2:2]
    slack = jnp.minimum(sizes[source_of] - 1, most - sizes[taker]) // 2
    slack = jnp.where((source_of == order[0]) | (taker == order[0]) | (sizes[taker] == 0), 0, jnp.maximum(slack, 0))
    moved = jax.random.randint(jax.random.fold_in(own, 4), (count // 2,), 0, 1 << 20) % (slack + 1)
    sizes = sizes.at[source_of].add(-moved).at[taker].add(moved)
    labels = jnp.searchsorted(jnp.cumsum(sizes), jnp.arange(rows * top), side="right").astype(jnp.int32)
    listing = labels.reshape(top, rows).T
    listing = listing[jax.random.permutation(jax.random.fold_in(own, 1), rows)]
    turn = jax.random.randint(jax.random.fold_in(own, 2), (rows, 1), 0, top)
    return jnp.take_along_axis(listing, (jnp.arange(top)[None, :] + turn) % top, axis=1)


def portions_of(number_of, total, bound, lean, full):
    loads = [(1 << 20) // math.isqrt(standing ** lean) + 1 for standing in range(1, number_of + 1)]
    largest = bound if full else min(bound, max(-(-total // number_of), total * loads[0] // sum(loads)))
    least = 1 if total - largest >= number_of - 1 else 0
    holding, rest = [largest] + [least] * (number_of - 1), total - largest - least * (number_of - 1)
    while rest > 0:
        movable = [i for i in range(1, number_of) if holding[i] < largest] or [i for i in range(1, number_of) if holding[i] < bound]
        whole, left = sum([loads[i] for i in movable]), rest
        for i in movable:
            addition = min(bound - holding[i], max(1, left * loads[i] // whole), rest)
            holding[i] = holding[i] + addition
            rest = rest - addition
    return np.array(holding)


def normal_values(key, shape, spread, limit, shards=(), held_as=jnp.bfloat16):
    factor_of = block_scale(key, shape, shards, -0.22, 0.18) if shards else 1.0
    drawn = jax.random.normal(key, shape, jnp.float32) * spread * factor_of
    return jnp.minimum(jnp.maximum(drawn, -limit), limit).astype(held_as)


def setup_inputs(seed: int = 0, part: int = 0) -> dict:
    seeds = jax.random.split(jax.random.key(seed), 9)
    part_splits = jax.random.split(jax.random.fold_in(seeds[8], part), 9)
    qkv = draw_qkv(jax.random.fold_in(jax.random.fold_in(seeds[8], part), 71), part)
    patches = draw_patches(jax.random.fold_in(jax.random.fold_in(seeds[8], part), 71), part)
    frame_starts = draw_frame_starts(jax.random.fold_in(jax.random.fold_in(seeds[8], part), 71), part)
    out_weight = normal_values(seeds[3], (D, D), D ** -0.5, 0.109375, ((1, 16),))
    layer_scale = jnp.clip(jnp.exp(jax.random.uniform(seeds[4], (D,), jnp.float32, math.log(0.5), math.log(5.0))), 0.5, 5.0)
    norm_gain = jnp.clip(1.0 + 0.18 * jax.random.normal(seeds[5], (4 * D,), jnp.float32), 0.1, 1.9)
    norm_bias = normal_values(seeds[6], (4 * D,), 0.5, 3.0, (), jnp.float32)
    owners_keys = jax.random.split(jax.random.fold_in(part_splits[7], 1), QUADS // QUAD_DEV)
    owners_turns = jax.random.permutation(jax.random.fold_in(part_splits[7], 3), QUADS // QUAD_DEV)
    owners = jax.vmap(lambda own, number: deal_out(jax.random.fold_in(part_splits[7], 2), own, number, QUAD_DEV, N_FSDP, 1, CAP, 2))(owners_keys, owners_turns).reshape((QUADS, 1))
    return {"qkv": qkv, "patches": patches, "frame_starts": frame_starts, "out_weight": out_weight, "layer_scale": layer_scale, "norm_gain": norm_gain, "norm_bias": norm_bias, "owners": owners}


def attend_block(operands):
    block_qkv, block_starts = operands
    frames = jnp.repeat(jnp.cumsum(block_starts), 4)
    queries = block_qkv[:, :D].reshape(TOK_DEV, HEADS, HEAD_DIM).astype(jnp.float32)
    key_heads = block_qkv[:, D:2 * D].reshape(TOK_DEV, HEADS, HEAD_DIM).astype(jnp.float32)
    value_heads = block_qkv[:, 2 * D:].reshape(TOK_DEV, HEADS, HEAD_DIM).astype(jnp.float32)
    scores = jnp.einsum('qhd,khd->hqk', queries, key_heads) * HEAD_DIM ** (-0.5)
    same_frame = frames[:, None] == frames[None, :]
    scores = jnp.where(same_frame[None], scores, -1e+30)
    row_max = lax.optimization_barrier(jnp.max(scores, axis=-1, keepdims=True))
    exps = jnp.exp(scores - row_max)
    weights = (exps / lax.optimization_barrier(jnp.sum(exps, axis=-1, keepdims=True))).astype(jnp.bfloat16)
    context = jnp.einsum('hqk,khd->qhd', weights.astype(jnp.float32), value_heads)
    return context.reshape(TOK_DEV, D).astype(jnp.bfloat16)

def layer_norm(merged, norm_gain, norm_bias):
    values = merged.astype(jnp.float32)
    centre = lax.optimization_barrier(jnp.mean(values, axis=-1, keepdims=True))
    centered = values - centre
    variance = lax.optimization_barrier(jnp.mean(centered * centered, axis=-1, keepdims=True))
    return centered * lax.rsqrt(variance + 1e-05) * norm_gain + norm_bias

def reference(qkv, patches, frame_starts, out_weight, layer_scale, norm_gain, norm_bias, owners):
    blocks = lax.map(attend_block, (qkv.reshape(N_FSDP, TOK_DEV, 3 * D), frame_starts.reshape(N_FSDP, QUAD_DEV)))
    context = blocks.reshape(TOKENS, D)
    projected = jnp.dot(context, out_weight, preferred_element_type=jnp.float32)
    layer_out = (patches.astype(jnp.float32) + layer_scale * projected).astype(jnp.bfloat16)
    merged = layer_out.reshape(QUADS, 4 * D)
    normed = layer_norm(merged, norm_gain, norm_bias).astype(jnp.bfloat16)
    owner_ids = owners[:, 0].astype(jnp.int32)
    one_hot = (owner_ids[:, None] == jnp.arange(N_FSDP, dtype=jnp.int32)[None, :]).astype(jnp.int32)
    one_hot = one_hot.reshape(N_FSDP, QUAD_DEV, N_FSDP)
    earlier = jnp.cumsum(one_hot, axis=1) - one_hot
    ranking = lax.optimization_barrier(jnp.sum(earlier * one_hot, axis=-1)).reshape(QUADS)
    source = jnp.arange(QUADS, dtype=jnp.int32) // QUAD_DEV
    slot_index = owner_ids * SLOTS + source * CAP + ranking
    owned = jnp.zeros((N_FSDP * SLOTS, 4 * D), jnp.bfloat16)
    return owned.at[slot_index].set(normed)
```

```python
import functools
import math

import jax
import jax.numpy as jnp
from jax import lax
from jax.experimental import pallas as pl
from jax.experimental.pallas import tpu as pltpu
from jax.sharding import PartitionSpec as P

HEADS = 25
MESH = pl.DeviceIdType.MESH
F32 = jnp.float32
BF16 = jnp.bfloat16


def dot_nt(a, b):
    return lax.dot_general(a, b, (((1,), (1,)), ((), ())), preferred_element_type=F32)


def kernel(
    n,
    cols,
    part,
    qkv,
    patches,
    starts_row,
    starts_col,
    w_own,
    scale,
    gain,
    bias,
    owners_row,
    owners_col,
    out,
    w_all,
    ctx,
    acc,
    layer_out,
    merged,
    slots,
    ring_send,
    ring_recv,
    swap_send,
    swap_recv,
    core_send,
    core_recv,
    core_swap_send,
    core_swap_recv,
    own_send,
    own_recv,
    out_send,
    out_recv,
    local_sem,
):
    tok, width = patches.shape
    head = width // HEADS
    quads = tok // 4
    cap = out.shape[1]
    padded = w_own.shape[0]
    chips = n // 2
    g = lax.axis_index("groups")
    f = lax.axis_index("fsdp")
    parity = lax.rem(g, 2)
    partner = g + 1 - 2 * parity
    core = lax.rem(f, 2)
    chip = f // 2
    sibling = f + 1 - 2 * core
    place = jnp.where(lax.rem(chip, 2) == 0, chip // 2, chips - 1 - chip // 2)
    sign = 1 - 2 * core
    steps = (chips // 2, chips - 1 - chips // 2)

    def chip_at(p):
        p = lax.rem(p + 2 * chips, chips)
        return jnp.where(p < chips // 2, 2 * p, 2 * (chips - 1 - p) + 1)

    def way(side):
        return sign if side == 0 else -sign

    def ring_shard(side, s):
        return chip_at(place - way(side) * s) * 2 + core

    def core_shard(side, s):
        return chip_at(place + way(side) * s) * 2 + (1 - core)

    ring_rows = pl.ds(pl.multiple_of(parity * part, 16), padded - part)
    mine_rows = pl.ds(pl.multiple_of(parity * (padded - part), 16), part)
    theirs_rows = pl.ds(pl.multiple_of((1 - parity) * (padded - part), 16), part)

    def remote(src, dst, send, recv, device):
        return pltpu.make_async_remote_copy(
            src_ref=src, dst_ref=dst, send_sem=send, recv_sem=recv, device_id=device, device_id_type=MESH
        )

    def ring_copy(side, s):
        ref = w_all.at[ring_shard(side, s), ring_rows]
        to = chip_at(place + way(side)) * 2 + core
        return remote(ref, ref, ring_send.at[side, s], ring_recv.at[side, s], (g, to))

    def ring_arrival(side, s):
        ref = w_all.at[ring_shard(side, s + 1), ring_rows]
        return remote(ref, ref, ring_send.at[side, s], ring_recv.at[side, s], (g, sibling))

    def swap_copy(side, s):
        ref = w_all.at[ring_shard(side, s + 1), mine_rows]
        return remote(ref, ref, swap_send.at[side, s], swap_recv.at[side, s], (partner, f))

    def swap_arrival(side, s):
        ref = w_all.at[ring_shard(side, s + 1), theirs_rows]
        return remote(ref, ref, swap_send.at[side, s], swap_recv.at[side, s], (partner, f))

    def core_copy(side, s):
        ref = w_all.at[ring_shard(side, s + 1), ring_rows]
        return remote(ref, ref, core_send.at[side, s], core_recv.at[side, s], (g, sibling))

    def core_arrival(side, s):
        ref = w_all.at[core_shard(side, s + 1), ring_rows]
        return remote(ref, ref, core_send.at[side, s], core_recv.at[side, s], (g, sibling))

    def core_swap_copy(side, s):
        ref = w_all.at[ring_shard(side, s + 1), theirs_rows]
        return remote(ref, ref, core_swap_send.at[side, s], core_swap_recv.at[side, s], (g, sibling))

    def core_swap_arrival(side, s):
        ref = w_all.at[core_shard(side, s + 1), theirs_rows]
        return remote(ref, ref, core_swap_send.at[side, s], core_swap_recv.at[side, s], (g, sibling))

    def out_copy(d):
        to = lax.rem(f + d, n)
        return remote(slots.at[to], out.at[f], out_send.at[d], out_recv.at[d], (g, to))

    def out_arrival(d):
        frm = lax.rem(f + n - d, n)
        return remote(slots.at[frm], out.at[frm], out_send.at[d], out_recv.at[d], (g, frm))

    barrier = pltpu.get_barrier_semaphore()

    @pl.loop(1, n)
    def _(d):
        pl.semaphore_signal(barrier, inc=1, device_id=(g, lax.rem(f + d, n)), device_id_type=MESH)

    pl.semaphore_signal(barrier, inc=1, device_id=(partner, f), device_id_type=MESH)
    pl.semaphore_wait(barrier, n)

    w_all[f] = w_own[...]
    ring_copy(0, 0).start()
    ring_copy(1, 0).start()
    own_out = remote(w_all.at[f], w_all.at[f], own_send, own_recv, (g, sibling))
    own_out.start()

    token = lax.broadcasted_iota(jnp.int32, (tok, quads), 0) // 4
    quad = lax.broadcasted_iota(jnp.int32, (tok, quads), 1)
    frame_q = jnp.sum(jnp.where(quad <= token, starts_row[...], 0).astype(F32), axis=1, keepdims=True)
    token = lax.broadcasted_iota(jnp.int32, (quads, tok), 1) // 4
    quad = lax.broadcasted_iota(jnp.int32, (quads, tok), 0)
    frame_k = jnp.sum(jnp.where(quad <= token, starts_col[...], 0).astype(F32), axis=0, keepdims=True)
    same = frame_q == frame_k
    factor = 1.0 / math.sqrt(head)

    def attend(h):
        at = pl.ds(pl.multiple_of(h * head, head), head)
        scores = dot_nt(qkv[:, at], qkv[:, pl.ds(pl.multiple_of(width + h * head, head), head)])
        scores = jnp.where(same, scores * factor, -1e30)
        exps = jnp.exp(scores - jnp.max(scores, axis=1, keepdims=True))
        total = jnp.sum(exps, axis=1, keepdims=True)
        weights = (exps / total).astype(BF16)
        values = qkv[:, pl.ds(pl.multiple_of(2 * width + h * head, head), head)]
        ctx[:, at] = jnp.dot(weights, values, preferred_element_type=F32).astype(BF16)

    @pl.loop(0, HEADS // 5)
    def _(i):
        for u in range(5):
            attend(i * 5 + u)

    def project(j):
        acc[j] = dot_nt(ctx[...], w_all[j])

    project(f)
    remote(w_all.at[sibling], w_all.at[sibling], own_send, own_recv, (g, sibling)).wait_recv()
    project(sibling)

    def receive(side, s):
        ring_arrival(side, s).wait_recv()

        @pl.when(s + 1 < steps[side])
        def _():
            ring_copy(side, s + 1).start()

        swap_copy(side, s).start()
        core_copy(side, s).start()

    def hand_on(side, s):
        swap_arrival(side, s).wait_recv()
        core_swap_copy(side, s).start()

    def finish(side, s):
        project(ring_shard(side, s + 1))
        core_arrival(side, s).wait_recv()
        core_swap_arrival(side, s).wait_recv()
        project(core_shard(side, s + 1))

    @pl.loop(0, steps[0] + 1)
    def _(s):
        for side in range(2):

            @pl.when(s < steps[side])
            def _():
                receive(side, s)

        for act in (hand_on, finish):
            for side in range(2):

                @pl.when(jnp.logical_and(s >= 1, s <= steps[side]))
                def _():
                    act(side, s - 1)

    for j in range(n):
        at = slice(j * cols, (j + 1) * cols)
        layer_out[:, at] = (patches[:, at].astype(F32) + scale[:, at] * acc[j][:, :cols]).astype(BF16)

    row = lax.broadcasted_iota(jnp.int32, (quads, tok), 0)
    column = lax.broadcasted_iota(jnp.int32, (quads, tok), 1)
    total = jnp.zeros((quads, 1), F32)
    for q in range(4):
        pick = (column == 4 * row + q).astype(BF16)
        values = jnp.dot(pick, layer_out[...], preferred_element_type=F32)
        merged[q] = values
        total += jnp.sum(values, axis=1, keepdims=True)
    centre = total / (4 * width)
    total = jnp.zeros((quads, 1), F32)
    for q in range(4):
        centered = merged[q] - centre
        total += jnp.sum(centered * centered, axis=1, keepdims=True)
    inverse = lax.rsqrt(total / (4 * width) + 1e-05)

    row = lax.broadcasted_iota(jnp.int32, (quads, quads), 0)
    column = lax.broadcasted_iota(jnp.int32, (quads, quads), 1)
    earlier = jnp.logical_and(owners_col[...] == owners_row[...], row < column)
    ranking = jnp.sum(earlier.astype(F32), axis=0, keepdims=True).astype(jnp.int32)
    target = owners_row[...] * cap + ranking
    place_of = (lax.broadcasted_iota(jnp.int32, (n * cap, quads), 0) == target).astype(BF16)
    for q in range(4):
        normed = ((merged[q] - centre) * inverse * gain[q : q + 1] + bias[q : q + 1]).astype(BF16)
        at = slice(q * width, (q + 1) * width)
        if cap % 8 == 0:
            routed = jnp.dot(place_of, normed, preferred_element_type=F32)
            slots[:, :, at] = routed.reshape(n, cap, width).astype(BF16)
        else:
            for d in range(n):
                routed = jnp.dot(place_of[d * cap : (d + 1) * cap], normed, preferred_element_type=F32)
                slots[d, :, at] = routed.astype(BF16)

    @pl.loop(1, n)
    def _(d):
        out_copy(d).start()

    own = pltpu.make_async_copy(slots.at[f], out.at[f], local_sem)
    own.start()

    own_out.wait_send()
    for side in range(2):

        @pl.loop(0, steps[side])
        def _(s):
            ring_copy(side, s).wait_send()
            swap_copy(side, s).wait_send()
            core_copy(side, s).wait_send()
            core_swap_copy(side, s).wait_send()

    own.wait()

    @pl.loop(1, n)
    def _(d):
        out_copy(d).wait_send()
        out_arrival(d).wait_recv()


def local(mesh, qkv, patches, frame_starts, out_weight, layer_scale, norm_gain, norm_bias, owners):
    n = mesh.shape["fsdp"]
    tok, width = patches.shape
    quads = tok // 4
    cols = out_weight.shape[1]
    padded = -(-cols // 16) * 16
    part = padded // 16 // 3 * 16
    cap = max(2, 2 * quads // n)
    chips = n // 2
    w_own = jnp.pad(out_weight.T, ((0, padded - cols), (0, 0)))
    vmem = pl.BlockSpec(memory_space=pltpu.VMEM)
    sems = pltpu.SemaphoreType.DMA((2, chips // 2))
    out = pl.pallas_call(
        functools.partial(kernel, n, cols, part),
        out_shape=jax.ShapeDtypeStruct((n, cap, 4 * width), BF16),
        in_specs=[vmem] * 10,
        out_specs=pl.BlockSpec(memory_space=pl.ANY),
        scratch_shapes=[
            pltpu.VMEM((n, padded, width), BF16),
            pltpu.VMEM((tok, width), BF16),
            pltpu.VMEM((n, tok, padded), F32),
            pltpu.VMEM((tok, width), BF16),
            pltpu.VMEM((4, quads, width), F32),
            pltpu.VMEM((n, cap, 4 * width), BF16),
        ]
        + [sems] * 8
        + [
            pltpu.SemaphoreType.DMA,
            pltpu.SemaphoreType.DMA,
            pltpu.SemaphoreType.DMA((n,)),
            pltpu.SemaphoreType.DMA((n,)),
            pltpu.SemaphoreType.DMA,
        ],
        compiler_params=pltpu.CompilerParams(
            collective_id=0, has_side_effects=True, vmem_limit_bytes=60 * 1024 * 1024
        ),
    )(
        qkv,
        patches,
        frame_starts.reshape(1, quads),
        frame_starts.reshape(quads, 1),
        w_own,
        layer_scale.reshape(1, width),
        norm_gain.reshape(4, width),
        norm_bias.reshape(4, width),
        owners.reshape(1, quads),
        owners,
    )
    return out.reshape(n * cap, 4 * width)


def solution(mesh):
    return jax.shard_map(
        functools.partial(local, mesh),
        mesh=mesh,
        in_specs=(
            P(("groups", "fsdp"), None),
            P(("groups", "fsdp"), None),
            P(("groups", "fsdp")),
            P(None, "fsdp"),
            P(),
            P(),
            P(),
            P(("groups", "fsdp"), None),
        ),
        out_specs=P(("groups", "fsdp"), None),
        check_vma=False,
    )
```

```python
import functools
import math

import jax
import jax.numpy as jnp
from jax import lax
from jax.experimental import pallas as pl
from jax.experimental.pallas import tpu as pltpu
from jax.sharding import PartitionSpec as P

HEADS = 25
MESH = pl.DeviceIdType.MESH
F32 = jnp.float32
BF16 = jnp.bfloat16


def dot_nt(a, b):
    return lax.dot_general(a, b, (((1,), (1,)), ((), ())), preferred_element_type=F32)


def kernel(
    n,
    cols,
    part,
    qkv_hbm,
    patches_hbm,
    starts_row,
    w_own,
    scale_tiles,
    gain_tiles,
    bias_tiles,
    owners_row,
    out,
    qkv,
    patches,
    scale,
    gain,
    bias,
    w_all,
    ctx,
    acc,
    layer_out,
    merged,
    slots,
    ring_send,
    ring_recv,
    swap_send,
    swap_recv,
    core_send,
    core_recv,
    core_swap_send,
    core_swap_recv,
    own_send,
    own_recv,
    out_send,
    out_recv,
    local_sem,
    qkv_sem,
    patches_sem,
):
    tok, width = patches.shape
    head = width // HEADS
    quads = tok // 4
    cap = out.shape[1]
    padded = w_all.shape[1]
    chips = n // 2
    g = lax.axis_index("groups")
    f = lax.axis_index("fsdp")
    parity = lax.rem(g, 2)
    partner = g + 1 - 2 * parity
    core = lax.rem(f, 2)
    chip = f // 2
    sibling = f + 1 - 2 * core
    place = jnp.where(lax.rem(chip, 2) == 0, chip // 2, chips - 1 - chip // 2)
    sign = 1 - 2 * core
    steps = (chips // 2, chips - 1 - chips // 2)

    def chip_at(p):
        p = lax.rem(p + 2 * chips, chips)
        return jnp.where(p < chips // 2, 2 * p, 2 * (chips - 1 - p) + 1)

    def way(side):
        return sign if side == 0 else -sign

    def ring_shard(side, s):
        return chip_at(place - way(side) * s) * 2 + core

    def core_shard(side, s):
        return chip_at(place + way(side) * s) * 2 + (1 - core)

    ring_rows = pl.ds(pl.multiple_of(parity * part, 16), padded - part)
    mine_rows = pl.ds(pl.multiple_of(parity * (padded - part), 16), part)
    theirs_rows = pl.ds(pl.multiple_of((1 - parity) * (padded - part), 16), part)

    def remote(src, dst, send, recv, device):
        return pltpu.make_async_remote_copy(
            src_ref=src, dst_ref=dst, send_sem=send, recv_sem=recv, device_id=device, device_id_type=MESH
        )

    def ring_copy(side, s):
        ref = w_all.at[ring_shard(side, s), ring_rows]
        to = chip_at(place + way(side)) * 2 + core
        return remote(ref, ref, ring_send.at[side, s], ring_recv.at[side, s], (g, to))

    def ring_arrival(side, s):
        ref = w_all.at[ring_shard(side, s + 1), ring_rows]
        return remote(ref, ref, ring_send.at[side, s], ring_recv.at[side, s], (g, sibling))

    def swap_copy(side, s):
        ref = w_all.at[ring_shard(side, s + 1), mine_rows]
        return remote(ref, ref, swap_send.at[side, s], swap_recv.at[side, s], (partner, f))

    def swap_arrival(side, s):
        ref = w_all.at[ring_shard(side, s + 1), theirs_rows]
        return remote(ref, ref, swap_send.at[side, s], swap_recv.at[side, s], (partner, f))

    def core_copy(side, s):
        ref = w_all.at[ring_shard(side, s + 1), ring_rows]
        return remote(ref, ref, core_send.at[side, s], core_recv.at[side, s], (g, sibling))

    def core_arrival(side, s):
        ref = w_all.at[core_shard(side, s + 1), ring_rows]
        return remote(ref, ref, core_send.at[side, s], core_recv.at[side, s], (g, sibling))

    def core_swap_copy(side, s):
        ref = w_all.at[ring_shard(side, s + 1), theirs_rows]
        return remote(ref, ref, core_swap_send.at[side, s], core_swap_recv.at[side, s], (g, sibling))

    def core_swap_arrival(side, s):
        ref = w_all.at[core_shard(side, s + 1), theirs_rows]
        return remote(ref, ref, core_swap_send.at[side, s], core_swap_recv.at[side, s], (g, sibling))

    def out_copy(d):
        to = lax.rem(f + d, n)
        return remote(slots.at[to], out.at[f], out_send.at[d], out_recv.at[d], (g, to))

    def out_arrival(d):
        frm = lax.rem(f + n - d, n)
        return remote(slots.at[frm], out.at[frm], out_send.at[d], out_recv.at[d], (g, frm))

    def as_column(row):
        size = row.shape[1]
        eye = lax.broadcasted_iota(jnp.int32, (size, size), 0) == lax.broadcasted_iota(
            jnp.int32, (size, size), 1
        )
        return jnp.sum(jnp.where(eye, row.astype(F32), 0.0), axis=1, keepdims=True)

    def unroll_tiles(tiles, rows):
        per_row = width // 128
        for q in range(rows.shape[0]):
            for t in range(per_row):
                at = q * per_row + t
                rows[q : q + 1, t * 128 : (t + 1) * 128] = tiles[at : at + 1, :]

    fetch_qkv = pltpu.make_async_copy(qkv_hbm, qkv, qkv_sem)
    fetch_qkv.start()
    fetch_patches = pltpu.make_async_copy(patches_hbm, patches, patches_sem)
    fetch_patches.start()

    barrier = pltpu.get_barrier_semaphore()

    @pl.loop(1, n)
    def _(d):
        pl.semaphore_signal(barrier, inc=1, device_id=(g, lax.rem(f + d, n)), device_id_type=MESH)

    pl.semaphore_signal(barrier, inc=1, device_id=(partner, f), device_id_type=MESH)
    pl.semaphore_wait(barrier, n)

    w_all[f, 0:cols] = w_own[...]
    if padded > cols:
        w_all[f, cols:padded] = jnp.zeros((padded - cols, width), BF16)
    ring_copy(0, 0).start()
    ring_copy(1, 0).start()
    own_out = remote(w_all.at[f], w_all.at[f], own_send, own_recv, (g, sibling))
    own_out.start()

    token = lax.broadcasted_iota(jnp.int32, (tok, quads), 0) // 4
    quad = lax.broadcasted_iota(jnp.int32, (tok, quads), 1)
    frame_q = jnp.sum(jnp.where(quad <= token, starts_row[...], 0).astype(F32), axis=1, keepdims=True)
    token = lax.broadcasted_iota(jnp.int32, (quads, tok), 1) // 4
    quad = lax.broadcasted_iota(jnp.int32, (quads, tok), 0)
    frame_k = jnp.sum(jnp.where(quad <= token, as_column(starts_row[...]), 0.0), axis=0, keepdims=True)
    same = frame_q == frame_k
    factor = 1.0 / math.sqrt(head)

    def attend(h):
        at = pl.ds(pl.multiple_of(h * head, head), head)
        scores = dot_nt(qkv[:, at], qkv[:, pl.ds(pl.multiple_of(width + h * head, head), head)])
        scores = jnp.where(same, scores * factor, -1e30)
        exps = jnp.exp(scores - jnp.max(scores, axis=1, keepdims=True))
        total = jnp.sum(exps, axis=1, keepdims=True)
        weights = (exps / total).astype(BF16)
        values = qkv[:, pl.ds(pl.multiple_of(2 * width + h * head, head), head)]
        ctx[:, at] = jnp.dot(weights, values, preferred_element_type=F32).astype(BF16)

    unroll_tiles(scale_tiles, scale)
    unroll_tiles(gain_tiles, gain)
    unroll_tiles(bias_tiles, bias)
    fetch_qkv.wait()

    @pl.loop(0, HEADS // 5)
    def _(i):
        for u in range(5):
            attend(i * 5 + u)

    def project(j):
        acc[j] = dot_nt(ctx[...], w_all[j])

    project(f)
    remote(w_all.at[sibling], w_all.at[sibling], own_send, own_recv, (g, sibling)).wait_recv()
    project(sibling)

    def receive(side, s):
        ring_arrival(side, s).wait_recv()

        @pl.when(s + 1 < steps[side])
        def _():
            ring_copy(side, s + 1).start()

        swap_copy(side, s).start()
        core_copy(side, s).start()

    def hand_on(side, s):
        swap_arrival(side, s).wait_recv()
        core_swap_copy(side, s).start()

    def finish(side, s):
        project(ring_shard(side, s + 1))
        core_arrival(side, s).wait_recv()
        core_swap_arrival(side, s).wait_recv()
        project(core_shard(side, s + 1))

    @pl.loop(0, steps[0] + 1)
    def _(s):
        for side in range(2):

            @pl.when(s < steps[side])
            def _():
                receive(side, s)

        for act in (hand_on, finish):
            for side in range(2):

                @pl.when(jnp.logical_and(s >= 1, s <= steps[side]))
                def _():
                    act(side, s - 1)

    fetch_patches.wait()
    for j in range(n):
        at = slice(j * cols, (j + 1) * cols)
        layer_out[:, at] = (patches[:, at].astype(F32) + scale[:, at] * acc[j][:, :cols]).astype(BF16)

    row = lax.broadcasted_iota(jnp.int32, (quads, tok), 0)
    column = lax.broadcasted_iota(jnp.int32, (quads, tok), 1)
    total = jnp.zeros((quads, 1), F32)
    for q in range(4):
        pick = (column == 4 * row + q).astype(BF16)
        values = jnp.dot(pick, layer_out[...], preferred_element_type=F32)
        merged[q] = values
        total += jnp.sum(values, axis=1, keepdims=True)
    centre = total / (4 * width)
    total = jnp.zeros((quads, 1), F32)
    for q in range(4):
        centered = merged[q] - centre
        total += jnp.sum(centered * centered, axis=1, keepdims=True)
    inverse = lax.rsqrt(total / (4 * width) + 1e-05)

    row = lax.broadcasted_iota(jnp.int32, (quads, quads), 0)
    column = lax.broadcasted_iota(jnp.int32, (quads, quads), 1)
    earlier = jnp.logical_and(as_column(owners_row[...]) == owners_row[...].astype(F32), row < column)
    ranking = jnp.sum(earlier.astype(F32), axis=0, keepdims=True).astype(jnp.int32)
    target = owners_row[...] * cap + ranking
    place_of = (lax.broadcasted_iota(jnp.int32, (n * cap, quads), 0) == target).astype(BF16)
    for q in range(4):
        normed = ((merged[q] - centre) * inverse * gain[q : q + 1] + bias[q : q + 1]).astype(BF16)
        at = slice(q * width, (q + 1) * width)
        if cap % 8 == 0:
            routed = jnp.dot(place_of, normed, preferred_element_type=F32)
            slots[:, :, at] = routed.reshape(n, cap, width).astype(BF16)
        else:
            for d in range(n):
                routed = jnp.dot(place_of[d * cap : (d + 1) * cap], normed, preferred_element_type=F32)
                slots[d, :, at] = routed.astype(BF16)

    @pl.loop(1, n)
    def _(d):
        out_copy(d).start()

    own = pltpu.make_async_copy(slots.at[f], out.at[f], local_sem)
    own.start()

    own_out.wait_send()
    for side in range(2):

        @pl.loop(0, steps[side])
        def _(s):
            ring_copy(side, s).wait_send()
            swap_copy(side, s).wait_send()
            core_copy(side, s).wait_send()
            core_swap_copy(side, s).wait_send()

    own.wait()

    @pl.loop(1, n)
    def _(d):
        out_copy(d).wait_send()
        out_arrival(d).wait_recv()


def local(mesh, qkv, patches, frame_starts, out_weight, layer_scale, norm_gain, norm_bias, owners):
    n = mesh.shape["fsdp"]
    tok, width = patches.shape
    quads = tok // 4
    cols = out_weight.shape[1]
    padded = -(-cols // 16) * 16
    part = padded // 16 // 3 * 16
    cap = max(2, 2 * quads // n)
    chips = n // 2
    vmem = pl.BlockSpec(memory_space=pltpu.VMEM)
    sems = pltpu.SemaphoreType.DMA((2, chips // 2))
    out = pl.pallas_call(
        functools.partial(kernel, n, cols, part),
        out_shape=jax.ShapeDtypeStruct((n, cap, 4 * width), BF16),
        in_specs=[pl.BlockSpec(memory_space=pl.ANY)] * 2 + [vmem] * 6,
        out_specs=pl.BlockSpec(memory_space=pl.ANY),
        scratch_shapes=[
            pltpu.VMEM(qkv.shape, BF16),
            pltpu.VMEM(patches.shape, BF16),
            pltpu.VMEM((1, width), F32),
            pltpu.VMEM((4, width), F32),
            pltpu.VMEM((4, width), F32),
            pltpu.VMEM((n, padded, width), BF16),
            pltpu.VMEM((tok, width), BF16),
            pltpu.VMEM((n, tok, padded), F32),
            pltpu.VMEM((tok, width), BF16),
            pltpu.VMEM((4, quads, width), F32),
            pltpu.VMEM((n, cap, 4 * width), BF16),
        ]
        + [sems] * 8
        + [
            pltpu.SemaphoreType.DMA,
            pltpu.SemaphoreType.DMA,
            pltpu.SemaphoreType.DMA((n,)),
            pltpu.SemaphoreType.DMA((n,)),
            pltpu.SemaphoreType.DMA,
            pltpu.SemaphoreType.DMA,
            pltpu.SemaphoreType.DMA,
        ],
        compiler_params=pltpu.CompilerParams(
            collective_id=0, has_side_effects=True, vmem_limit_bytes=60 * 1024 * 1024
        ),
    )(
        qkv,
        patches,
        frame_starts.reshape(1, quads),
        out_weight.T,
        layer_scale.reshape(width // 128, 128),
        norm_gain.reshape(4 * width // 128, 128),
        norm_bias.reshape(4 * width // 128, 128),
        owners.reshape(1, quads),
    )
    return out.reshape(n * cap, 4 * width)


def solution(mesh):
    return jax.shard_map(
        functools.partial(local, mesh),
        mesh=mesh,
        in_specs=(
            P(("groups", "fsdp"), None),
            P(("groups", "fsdp"), None),
            P(("groups", "fsdp")),
            P(None, "fsdp"),
            P(),
            P(),
            P(),
            P(("groups", "fsdp"), None),
        ),
        out_specs=P(("groups", "fsdp"), None),
        check_vma=False,
    )
```

```python
import functools
import math

import jax
import jax.numpy as jnp
from jax import lax
from jax.experimental import pallas as pl
from jax.experimental.pallas import tpu as pltpu
from jax.sharding import PartitionSpec as P

HEADS = 25
MESH = pl.DeviceIdType.MESH
F32 = jnp.float32
BF16 = jnp.bfloat16


def dot_nt(a, b):
    return lax.dot_general(a, b, (((1,), (1,)), ((), ())), preferred_element_type=F32)


def kernel(
    n,
    cols,
    part,
    qkv_hbm,
    patches_hbm,
    starts_row,
    w_own,
    scale_tiles,
    gain_tiles,
    bias_tiles,
    owners_row,
    out,
    qkv,
    patches,
    scale,
    gain,
    bias,
    w_all,
    ctx,
    acc,
    layer_out,
    merged,
    slots,
    ring_send,
    ring_recv,
    swap_send,
    swap_recv,
    core_send,
    core_recv,
    core_swap_send,
    core_swap_recv,
    own_send,
    own_recv,
    out_send,
    out_recv,
    local_sem,
    qkv_sem,
    patches_sem,
):
    tok, width = patches.shape
    head = width // HEADS
    quads = tok // 4
    cap = out.shape[1]
    padded = w_all.shape[1]
    chips = n // 2
    g = lax.axis_index("groups")
    f = lax.axis_index("fsdp")
    parity = lax.rem(g, 2)
    partner = g + 1 - 2 * parity
    core = lax.rem(f, 2)
    chip = f // 2
    sibling = f + 1 - 2 * core
    place = jnp.where(lax.rem(chip, 2) == 0, chip // 2, chips - 1 - chip // 2)
    sign = 1 - 2 * core
    steps = (chips // 2, chips - 1 - chips // 2)

    def chip_at(p):
        p = lax.rem(p + 2 * chips, chips)
        return jnp.where(p < chips // 2, 2 * p, 2 * (chips - 1 - p) + 1)

    def way(side):
        return sign if side == 0 else -sign

    def ring_shard(side, s):
        return chip_at(place - way(side) * s) * 2 + core

    def core_shard(side, s):
        return chip_at(place + way(side) * s) * 2 + (1 - core)

    ring_rows = pl.ds(pl.multiple_of(parity * part, 16), padded - part)
    mine_rows = pl.ds(pl.multiple_of(parity * (padded - part), 16), part)
    theirs_rows = pl.ds(pl.multiple_of((1 - parity) * (padded - part), 16), part)

    def remote(src, dst, send, recv, device):
        return pltpu.make_async_remote_copy(
            src_ref=src, dst_ref=dst, send_sem=send, recv_sem=recv, device_id=device, device_id_type=MESH
        )

    def ring_copy(side, s):
        ref = w_all.at[ring_shard(side, s), ring_rows]
        to = chip_at(place + way(side)) * 2 + core
        return remote(ref, ref, ring_send.at[side, s], ring_recv.at[side, s], (g, to))

    def ring_arrival(side, s):
        ref = w_all.at[ring_shard(side, s + 1), ring_rows]
        return remote(ref, ref, ring_send.at[side, s], ring_recv.at[side, s], (g, sibling))

    def swap_copy(side, s):
        ref = w_all.at[ring_shard(side, s + 1), mine_rows]
        return remote(ref, ref, swap_send.at[side, s], swap_recv.at[side, s], (partner, f))

    def swap_arrival(side, s):
        ref = w_all.at[ring_shard(side, s + 1), theirs_rows]
        return remote(ref, ref, swap_send.at[side, s], swap_recv.at[side, s], (partner, f))

    def core_copy(side, s):
        ref = w_all.at[ring_shard(side, s + 1), ring_rows]
        return remote(ref, ref, core_send.at[side, s], core_recv.at[side, s], (g, sibling))

    def core_arrival(side, s):
        ref = w_all.at[core_shard(side, s + 1), ring_rows]
        return remote(ref, ref, core_send.at[side, s], core_recv.at[side, s], (g, sibling))

    def core_swap_copy(side, s):
        ref = w_all.at[ring_shard(side, s + 1), theirs_rows]
        return remote(ref, ref, core_swap_send.at[side, s], core_swap_recv.at[side, s], (g, sibling))

    def core_swap_arrival(side, s):
        ref = w_all.at[core_shard(side, s + 1), theirs_rows]
        return remote(ref, ref, core_swap_send.at[side, s], core_swap_recv.at[side, s], (g, sibling))

    def out_copy(d):
        to = lax.rem(f + d, n)
        return remote(slots.at[to], out.at[f], out_send.at[d], out_recv.at[d], (g, to))

    def out_arrival(d):
        frm = lax.rem(f + n - d, n)
        return remote(slots.at[frm], out.at[frm], out_send.at[d], out_recv.at[d], (g, frm))

    def as_column(row):
        size = row.shape[1]
        eye = lax.broadcasted_iota(jnp.int32, (size, size), 0) == lax.broadcasted_iota(
            jnp.int32, (size, size), 1
        )
        return jnp.sum(jnp.where(eye, row.astype(F32), 0.0), axis=1, keepdims=True)

    def unroll_tiles(tiles, rows):
        per_row = width // 128
        for q in range(rows.shape[0]):
            for t in range(per_row):
                at = q * per_row + t
                rows[q : q + 1, t * 128 : (t + 1) * 128] = tiles[at : at + 1, :]

    fetch_qkv = pltpu.make_async_copy(qkv_hbm, qkv, qkv_sem)
    fetch_qkv.start()
    fetch_patches = pltpu.make_async_copy(patches_hbm, patches, patches_sem)
    fetch_patches.start()

    barrier = pltpu.get_barrier_semaphore()

    @pl.loop(1, n)
    def _(d):
        pl.semaphore_signal(barrier, inc=1, device_id=(g, lax.rem(f + d, n)), device_id_type=MESH)

    pl.semaphore_signal(barrier, inc=1, device_id=(partner, f), device_id_type=MESH)
    pl.semaphore_wait(barrier, n)

    w_all[f, 0:cols] = w_own[...]
    if padded > cols:
        w_all[f, cols:padded] = jnp.zeros((padded - cols, width), BF16)
    ring_copy(0, 0).start()
    ring_copy(1, 0).start()
    own_out = remote(w_all.at[f], w_all.at[f], own_send, own_recv, (g, sibling))
    own_out.start()

    token = lax.broadcasted_iota(jnp.int32, (tok, quads), 0) // 4
    quad = lax.broadcasted_iota(jnp.int32, (tok, quads), 1)
    frame_q = jnp.sum(jnp.where(quad <= token, starts_row[...], 0).astype(F32), axis=1, keepdims=True)
    token = lax.broadcasted_iota(jnp.int32, (quads, tok), 1) // 4
    quad = lax.broadcasted_iota(jnp.int32, (quads, tok), 0)
    frame_k = jnp.sum(jnp.where(quad <= token, as_column(starts_row[...]), 0.0), axis=0, keepdims=True)
    same = frame_q == frame_k
    factor = 1.0 / math.sqrt(head)

    def attend(h):
        at = pl.ds(pl.multiple_of(h * head, head), head)
        scores = dot_nt(qkv[:, at], qkv[:, pl.ds(pl.multiple_of(width + h * head, head), head)])
        scores = jnp.where(same, scores * factor, -1e30)
        exps = jnp.exp(scores - jnp.max(scores, axis=1, keepdims=True))
        total = jnp.sum(exps, axis=1, keepdims=True)
        weights = (exps / total).astype(BF16)
        values = qkv[:, pl.ds(pl.multiple_of(2 * width + h * head, head), head)]
        ctx[:, at] = jnp.dot(weights, values, preferred_element_type=F32).astype(BF16)

    unroll_tiles(scale_tiles, scale)
    unroll_tiles(gain_tiles, gain)
    unroll_tiles(bias_tiles, bias)
    fetch_qkv.wait()

    @pl.loop(0, HEADS // 5)
    def _(i):
        for u in range(5):
            attend(i * 5 + u)

    def project(j):
        acc[j] = dot_nt(ctx[...], w_all[j])

    project(f)
    remote(w_all.at[sibling], w_all.at[sibling], own_send, own_recv, (g, sibling)).wait_recv()
    project(sibling)

    def receive(side, s):
        ring_arrival(side, s).wait_recv()

        @pl.when(s + 1 < steps[side])
        def _():
            ring_copy(side, s + 1).start()

        swap_copy(side, s).start()
        core_copy(side, s).start()

    def hand_on(side, s):
        swap_arrival(side, s).wait_recv()
        core_swap_copy(side, s).start()

    def finish(side, s):
        project(ring_shard(side, s + 1))
        core_arrival(side, s).wait_recv()
        core_swap_arrival(side, s).wait_recv()
        project(core_shard(side, s + 1))

    @pl.loop(0, steps[0] + 1)
    def _(s):
        for side in range(2):

            @pl.when(s < steps[side])
            def _():
                receive(side, s)

        for act in (hand_on, finish):
            for side in range(2):

                @pl.when(jnp.logical_and(s >= 1, s <= steps[side]))
                def _():
                    act(side, s - 1)

    fetch_patches.wait()
    for j in range(n):
        at = slice(j * cols, (j + 1) * cols)
        layer_out[:, at] = (patches[:, at].astype(F32) + scale[:, at] * acc[j][:, :cols]).astype(BF16)

    row = lax.broadcasted_iota(jnp.int32, (quads, tok), 0)
    column = lax.broadcasted_iota(jnp.int32, (quads, tok), 1)
    total = jnp.zeros((quads, 1), F32)
    for q in range(4):
        pick = (column == 4 * row + q).astype(BF16)
        values = jnp.dot(pick, layer_out[...], preferred_element_type=F32)
        merged[q] = values
        total += jnp.sum(values, axis=1, keepdims=True)
    centre = total / (4 * width)
    total = jnp.zeros((quads, 1), F32)
    for q in range(4):
        centered = merged[q] - centre
        total += jnp.sum(centered * centered, axis=1, keepdims=True)
    inverse = lax.rsqrt(total / (4 * width) + 1e-05)

    row = lax.broadcasted_iota(jnp.int32, (quads, quads), 0)
    column = lax.broadcasted_iota(jnp.int32, (quads, quads), 1)
    earlier = jnp.logical_and(as_column(owners_row[...]) == owners_row[...].astype(F32), row < column)
    ranking = jnp.sum(earlier.astype(F32), axis=0, keepdims=True).astype(jnp.int32)
    target = owners_row[...] * cap + ranking
    place_of = (lax.broadcasted_iota(jnp.int32, (n * cap, quads), 0) == target).astype(BF16)
    for q in range(4):
        normed = ((merged[q] - centre) * inverse * gain[q : q + 1] + bias[q : q + 1]).astype(BF16)
        at = slice(q * width, (q + 1) * width)
        if cap % 8 == 0:
            routed = jnp.dot(place_of, normed, preferred_element_type=F32)
            slots[:, :, at] = routed.reshape(n, cap, width).astype(BF16)
        else:
            for d in range(n):
                routed = jnp.dot(place_of[d * cap : (d + 1) * cap], normed, preferred_element_type=F32)
                slots[d, :, at] = routed.astype(BF16)

    @pl.loop(1, n)
    def _(d):
        out_copy(d).start()

    own = pltpu.make_async_copy(slots.at[f], out.at[f], local_sem)
    own.start()

    own_out.wait_send()
    for side in range(2):

        @pl.loop(0, steps[side])
        def _(s):
            ring_copy(side, s).wait_send()
            swap_copy(side, s).wait_send()
            core_copy(side, s).wait_send()
            core_swap_copy(side, s).wait_send()

    own.wait()

    @pl.loop(1, n)
    def _(d):
        out_copy(d).wait_send()
        out_arrival(d).wait_recv()


def overlapped_kernel(
    n,
    cols,
    part,
    qkv_hbm,
    patches_hbm,
    starts_row,
    w_own,
    scale_tiles,
    gain_tiles,
    bias_tiles,
    owners_row,
    out,
    qkv,
    patches,
    scale,
    gain,
    bias,
    w_all,
    ctx,
    acc,
    patch_chunks,
    scale_chunks,
    merged,
    slots,
    route,
    first_out,
    second_out,
    flags_out,
    first_in,
    second_in,
    flags_in,
    ring_send,
    ring_recv,
    swap_send,
    swap_recv,
    core_send,
    core_recv,
    core_swap_send,
    core_swap_recv,
    own_send,
    own_recv,
    first_send,
    first_recv,
    second_send,
    second_recv,
    flags_send,
    flags_recv,
    local_sem,
    qkv_sem,
    patches_sem,
):
    tok, width = patches.shape
    head = width // HEADS
    quads = tok // 4
    cap = out.shape[0] // n
    padded = w_all.shape[1]
    chips = n // 2
    g = lax.axis_index("groups")
    f = lax.axis_index("fsdp")
    parity = lax.rem(g, 2)
    partner = g + 1 - 2 * parity
    core = lax.rem(f, 2)
    chip = f // 2
    sibling = f + 1 - 2 * core
    place = jnp.where(lax.rem(chip, 2) == 0, chip // 2, chips - 1 - chip // 2)
    sign = 1 - 2 * core
    steps = (chips // 2, chips - 1 - chips // 2)

    def chip_at(p):
        p = lax.rem(p + 2 * chips, chips)
        return jnp.where(p < chips // 2, 2 * p, 2 * (chips - 1 - p) + 1)

    def way(side):
        return sign if side == 0 else -sign

    def ring_shard(side, s):
        return chip_at(place - way(side) * s) * 2 + core

    def core_shard(side, s):
        return chip_at(place + way(side) * s) * 2 + (1 - core)

    ring_rows = pl.ds(pl.multiple_of(parity * part, 16), padded - part)
    mine_rows = pl.ds(pl.multiple_of(parity * (padded - part), 16), part)
    theirs_rows = pl.ds(pl.multiple_of((1 - parity) * (padded - part), 16), part)

    def remote(src, dst, send, recv, device):
        return pltpu.make_async_remote_copy(
            src_ref=src, dst_ref=dst, send_sem=send, recv_sem=recv, device_id=device, device_id_type=MESH
        )

    def ring_copy(side, s):
        ref = w_all.at[ring_shard(side, s), ring_rows]
        to = chip_at(place + way(side)) * 2 + core
        return remote(ref, ref, ring_send.at[side, s], ring_recv.at[side, s], (g, to))

    def ring_arrival(side, s):
        ref = w_all.at[ring_shard(side, s + 1), ring_rows]
        return remote(ref, ref, ring_send.at[side, s], ring_recv.at[side, s], (g, sibling))

    def swap_copy(side, s):
        ref = w_all.at[ring_shard(side, s + 1), mine_rows]
        return remote(ref, ref, swap_send.at[side, s], swap_recv.at[side, s], (partner, f))

    def swap_arrival(side, s):
        ref = w_all.at[ring_shard(side, s + 1), theirs_rows]
        return remote(ref, ref, swap_send.at[side, s], swap_recv.at[side, s], (partner, f))

    def core_copy(side, s):
        ref = w_all.at[ring_shard(side, s + 1), ring_rows]
        return remote(ref, ref, core_send.at[side, s], core_recv.at[side, s], (g, sibling))

    def core_arrival(side, s):
        ref = w_all.at[core_shard(side, s + 1), ring_rows]
        return remote(ref, ref, core_send.at[side, s], core_recv.at[side, s], (g, sibling))

    def core_swap_copy(side, s):
        ref = w_all.at[ring_shard(side, s + 1), theirs_rows]
        return remote(ref, ref, core_swap_send.at[side, s], core_swap_recv.at[side, s], (g, sibling))

    def core_swap_arrival(side, s):
        ref = w_all.at[core_shard(side, s + 1), theirs_rows]
        return remote(ref, ref, core_swap_send.at[side, s], core_swap_recv.at[side, s], (g, sibling))

    first = (first_out, first_in, first_send, first_recv)
    second = (second_out, second_in, second_send, second_recv)
    flags = (flags_out, flags_in, flags_send, flags_recv)

    def out_copy(group, d):
        source, target, send, recv = group
        to = lax.rem(f + d, n)
        return remote(source.at[to], target.at[f], send.at[d], recv.at[d], (g, to))

    def out_arrival(group, d):
        source, target, send, recv = group
        frm = lax.rem(f + n - d, n)
        return remote(source.at[frm], target.at[frm], send.at[d], recv.at[d], (g, frm))

    def send_out(group):
        source, target = group[:2]

        @pl.loop(1, n)
        def _(d):
            out_copy(group, d).start()

        target[f] = source[f]

    def place_in_ring(c):
        return c // 2 if c % 2 == 0 else chips - 1 - c // 2

    def chip_of_place(p):
        p = p % chips
        return 2 * p if p < chips // 2 else 2 * (chips - 1 - p) + 1

    mid = chips // 4
    early = [0] + [r for s in range(1, mid + 1) for r in (s, -s)]
    late = [r for s in range(mid + 1, chips // 2) for r in (s, -s)] + [chips // 2]
    wide = 2 * cols

    def as_column(row):
        size = row.shape[1]
        eye = lax.broadcasted_iota(jnp.int32, (size, size), 0) == lax.broadcasted_iota(
            jnp.int32, (size, size), 1
        )
        return jnp.sum(jnp.where(eye, row.astype(F32), 0.0), axis=1, keepdims=True)

    def unroll_tiles(tiles, rows):
        per_row = width // 128
        for q in range(rows.shape[0]):
            for t in range(per_row):
                at = q * per_row + t
                rows[q : q + 1, t * 128 : (t + 1) * 128] = tiles[at : at + 1, :]

    fetch_qkv = pltpu.make_async_copy(qkv_hbm, qkv, qkv_sem)
    fetch_qkv.start()
    fetch_patches = pltpu.make_async_copy(patches_hbm, patches, patches_sem)
    fetch_patches.start()

    barrier = pltpu.get_barrier_semaphore()

    @pl.loop(1, n)
    def _(d):
        pl.semaphore_signal(barrier, inc=1, device_id=(g, lax.rem(f + d, n)), device_id_type=MESH)

    pl.semaphore_signal(barrier, inc=1, device_id=(partner, f), device_id_type=MESH)
    pl.semaphore_wait(barrier, n)

    w_all[f, 0:cols] = w_own[...]
    if padded > cols:
        w_all[f, cols:padded] = jnp.zeros((padded - cols, width), BF16)
    ring_copy(0, 0).start()
    ring_copy(1, 0).start()
    own_out = remote(w_all.at[f], w_all.at[f], own_send, own_recv, (g, sibling))
    own_out.start()

    token = lax.broadcasted_iota(jnp.int32, (tok, quads), 0) // 4
    quad = lax.broadcasted_iota(jnp.int32, (tok, quads), 1)
    frame_q = jnp.sum(jnp.where(quad <= token, starts_row[...], 0).astype(F32), axis=1, keepdims=True)
    token = lax.broadcasted_iota(jnp.int32, (quads, tok), 1) // 4
    quad = lax.broadcasted_iota(jnp.int32, (quads, tok), 0)
    frame_k = jnp.sum(jnp.where(quad <= token, as_column(starts_row[...]), 0.0), axis=0, keepdims=True)
    same = frame_q == frame_k
    factor = 1.0 / math.sqrt(head)

    def attend(h):
        at = pl.ds(pl.multiple_of(h * head, head), head)
        scores = dot_nt(qkv[:, at], qkv[:, pl.ds(pl.multiple_of(width + h * head, head), head)])
        scores = jnp.where(same, scores * factor, -1e30)
        exps = jnp.exp(scores - jnp.max(scores, axis=1, keepdims=True))
        total = jnp.sum(exps, axis=1, keepdims=True)
        weights = (exps / total).astype(BF16)
        values = qkv[:, pl.ds(pl.multiple_of(2 * width + h * head, head), head)]
        ctx[:, at] = jnp.dot(weights, values, preferred_element_type=F32).astype(BF16)

    unroll_tiles(scale_tiles, scale)
    unroll_tiles(gain_tiles, gain)
    unroll_tiles(bias_tiles, bias)
    fetch_qkv.wait()

    @pl.loop(0, HEADS // 5)
    def _(i):
        for u in range(5):
            attend(i * 5 + u)

    fetch_patches.wait()
    for c in range(chips):
        at = slice(c * wide, (c + 1) * wide)
        patch_chunks[c, :, :wide] = patches[:, at]
        scale_chunks[c, :, :wide] = scale[:, at]

    row = lax.broadcasted_iota(jnp.int32, (quads, quads), 0)
    column = lax.broadcasted_iota(jnp.int32, (quads, quads), 1)
    earlier = jnp.logical_and(as_column(owners_row[...]) == owners_row[...].astype(F32), row < column)
    ranking = jnp.sum(earlier.astype(F32), axis=0, keepdims=True)
    target = owners_row[...].astype(F32) * cap + ranking
    filled = lax.broadcasted_iota(jnp.int32, (n * cap, quads), 0).astype(F32) == target
    filled = jnp.sum(filled.astype(F32), axis=1, keepdims=True)
    flags_out[...] = jnp.broadcast_to(filled, (n * cap, 128)).reshape(n, cap, 128)
    token_target = jnp.sum(jnp.where(quad == token, as_column(target), 0.0), axis=0, keepdims=True)
    row = lax.broadcasted_iota(jnp.int32, (4 * n * cap, tok), 0)
    column = lax.broadcasted_iota(jnp.int32, (4 * n * cap, tok), 1)
    slot = row // (4 * cap) * cap + lax.rem(row, cap)
    part_of = lax.rem(row // cap, 4) == lax.rem(column, 4)
    route[...] = jnp.logical_and(slot.astype(F32) == token_target, part_of).astype(BF16)

    def pack(places, target):
        for i, r in enumerate(places):
            c = chip_at(place + r)
            projected = jnp.concatenate([acc[2 * c][:, :cols], acc[2 * c + 1][:, :cols]], axis=1)
            values = patch_chunks[c][:, :wide].astype(F32) + scale_chunks[c][:, :wide] * projected
            routed = jnp.dot(route[...], values.astype(BF16), preferred_element_type=F32)
            target[:, :, i * wide : (i + 1) * wide] = routed.reshape(n, 4 * cap, wide).astype(BF16)

    def project(j):
        acc[j] = dot_nt(ctx[...], w_all[j])

    project(f)
    remote(w_all.at[sibling], w_all.at[sibling], own_send, own_recv, (g, sibling)).wait_recv()
    project(sibling)

    def receive(side, s):
        ring_arrival(side, s).wait_recv()

        @pl.when(s + 1 < steps[side])
        def _():
            ring_copy(side, s + 1).start()

        swap_copy(side, s).start()
        core_copy(side, s).start()

    def hand_on(side, s):
        swap_arrival(side, s).wait_recv()
        core_swap_copy(side, s).start()

    def finish(side, s):
        project(ring_shard(side, s + 1))
        core_arrival(side, s).wait_recv()
        core_swap_arrival(side, s).wait_recv()
        project(core_shard(side, s + 1))

    def turn(s):
        for side in range(2):

            @pl.when(s < steps[side])
            def _():
                receive(side, s)

        for act in (hand_on, finish):
            for side in range(2):

                @pl.when(jnp.logical_and(s >= 1, s <= steps[side]))
                def _():
                    act(side, s - 1)

    pl.loop(0, mid + 1)(turn)
    pack(early, first_out)
    send_out(first)
    send_out(flags)
    pl.loop(mid + 1, steps[0] + 1)(turn)
    pack(late, second_out)
    send_out(second)

    own_out.wait_send()
    for side in range(2):

        @pl.loop(0, steps[side])
        def _(s):
            ring_copy(side, s).wait_send()
            swap_copy(side, s).wait_send()
            core_copy(side, s).wait_send()
            core_swap_copy(side, s).wait_send()

    def collect(group, places):
        @pl.loop(1, n)
        def _(d):
            out_copy(group, d).wait_send()
            out_arrival(group, d).wait_recv()

        for src in range(n):
            for i, r in enumerate(places):
                c = chip_of_place(place_in_ring(src // 2) + r)
                values = group[1][src, :, i * wide : (i + 1) * wide]
                for q in range(4):
                    merged[q, src * cap : (src + 1) * cap, c * wide : (c + 1) * wide] = values[
                        q * cap : (q + 1) * cap
                    ]

    collect(first, early)
    collect(flags, [])
    collect(second, late)

    def over_parts(step):
        return lax.fori_loop(0, 4, step, jnp.zeros((n * cap, 1), F32))

    def add_values(q, total):
        return total + jnp.sum(merged[q].astype(F32), axis=1, keepdims=True)

    centre = over_parts(add_values) / (4 * width)

    def add_squares(q, total):
        centered = merged[q].astype(F32) - centre
        return total + jnp.sum(centered * centered, axis=1, keepdims=True)

    inverse = lax.rsqrt(over_parts(add_squares) / (4 * width) + 1e-05)
    present = flags_in[...].reshape(n * cap, 128)[:, :1] > 0.5

    @pl.loop(0, 4)
    def _(q):
        values = merged[q].astype(F32)
        normed = (values - centre) * inverse * gain[pl.ds(q, 1)] + bias[pl.ds(q, 1)]
        normed = jnp.where(present, normed, 0.0).astype(BF16)
        slots[:, pl.ds(pl.multiple_of(q * width, 128), width)] = normed

    own = pltpu.make_async_copy(slots, out, local_sem)
    own.start()
    own.wait()


def overlapped(n, cols, padded, part, cap, qkv, patches, frame_starts, out_weight, layer_scale, norm_gain, norm_bias, owners):
    tok, width = patches.shape
    quads = tok // 4
    chips = n // 2
    mid = chips // 4
    early = -(-(2 * mid + 1) * 2 * cols // 128) * 128
    late = -(-(chips - 2 * mid - 1) * 2 * cols // 128) * 128
    vmem = pl.BlockSpec(memory_space=pltpu.VMEM)
    sems = pltpu.SemaphoreType.DMA((2, chips // 2))
    one = pltpu.SemaphoreType.DMA
    each = pltpu.SemaphoreType.DMA((n,))
    exchange = [
        pltpu.VMEM((n, 4 * cap, early), BF16),
        pltpu.VMEM((n, 4 * cap, late), BF16),
        pltpu.VMEM((n, cap, 128), F32),
    ]
    return pl.pallas_call(
        functools.partial(overlapped_kernel, n, cols, part),
        out_shape=jax.ShapeDtypeStruct((n * cap, 4 * width), BF16),
        in_specs=[pl.BlockSpec(memory_space=pl.ANY)] * 2 + [vmem] * 6,
        out_specs=pl.BlockSpec(memory_space=pl.ANY),
        scratch_shapes=[
            pltpu.VMEM(qkv.shape, BF16),
            pltpu.VMEM(patches.shape, BF16),
            pltpu.VMEM((1, width), F32),
            pltpu.VMEM((4, width), F32),
            pltpu.VMEM((4, width), F32),
            pltpu.VMEM((n, padded, width), BF16),
            pltpu.VMEM((tok, width), BF16),
            pltpu.VMEM((n, tok, padded), F32),
            pltpu.VMEM((chips, tok, 2 * cols), BF16),
            pltpu.VMEM((chips, 1, 2 * cols), F32),
            pltpu.VMEM((4, n * cap, width), BF16),
            pltpu.VMEM((n * cap, 4 * width), BF16),
            pltpu.VMEM((4 * n * cap, tok), BF16),
        ]
        + exchange * 2
        + [sems] * 8
        + [one] * 2
        + [each] * 6
        + [one] * 3,
        compiler_params=pltpu.CompilerParams(
            collective_id=1, has_side_effects=True, vmem_limit_bytes=62 * 1024 * 1024
        ),
    )(
        qkv,
        patches,
        frame_starts.reshape(1, quads),
        out_weight.T,
        layer_scale.reshape(width // 128, 128),
        norm_gain.reshape(4 * width // 128, 128),
        norm_bias.reshape(4 * width // 128, 128),
        owners.reshape(1, quads),
    )


def local(mesh, qkv, patches, frame_starts, out_weight, layer_scale, norm_gain, norm_bias, owners):
    n = mesh.shape["fsdp"]
    tok, width = patches.shape
    quads = tok // 4
    cols = out_weight.shape[1]
    padded = -(-cols // 16) * 16
    part = padded // 16 // 3 * 16
    cap = max(2, 2 * quads // n)
    chips = n // 2
    vmem = pl.BlockSpec(memory_space=pltpu.VMEM)
    sems = pltpu.SemaphoreType.DMA((2, chips // 2))
    if cap % 8 == 0 and chips % 4 == 0:
        return overlapped(n, cols, padded, part, cap, qkv, patches, frame_starts, out_weight, layer_scale, norm_gain, norm_bias, owners)
    out = pl.pallas_call(
        functools.partial(kernel, n, cols, part),
        out_shape=jax.ShapeDtypeStruct((n, cap, 4 * width), BF16),
        in_specs=[pl.BlockSpec(memory_space=pl.ANY)] * 2 + [vmem] * 6,
        out_specs=pl.BlockSpec(memory_space=pl.ANY),
        scratch_shapes=[
            pltpu.VMEM(qkv.shape, BF16),
            pltpu.VMEM(patches.shape, BF16),
            pltpu.VMEM((1, width), F32),
            pltpu.VMEM((4, width), F32),
            pltpu.VMEM((4, width), F32),
            pltpu.VMEM((n, padded, width), BF16),
            pltpu.VMEM((tok, width), BF16),
            pltpu.VMEM((n, tok, padded), F32),
            pltpu.VMEM((tok, width), BF16),
            pltpu.VMEM((4, quads, width), F32),
            pltpu.VMEM((n, cap, 4 * width), BF16),
        ]
        + [sems] * 8
        + [
            pltpu.SemaphoreType.DMA,
            pltpu.SemaphoreType.DMA,
            pltpu.SemaphoreType.DMA((n,)),
            pltpu.SemaphoreType.DMA((n,)),
            pltpu.SemaphoreType.DMA,
            pltpu.SemaphoreType.DMA,
            pltpu.SemaphoreType.DMA,
        ],
        compiler_params=pltpu.CompilerParams(
            collective_id=0, has_side_effects=True, vmem_limit_bytes=60 * 1024 * 1024
        ),
    )(
        qkv,
        patches,
        frame_starts.reshape(1, quads),
        out_weight.T,
        layer_scale.reshape(width // 128, 128),
        norm_gain.reshape(4 * width // 128, 128),
        norm_bias.reshape(4 * width // 128, 128),
        owners.reshape(1, quads),
    )
    return out.reshape(n * cap, 4 * width)


def solution(mesh):
    return jax.shard_map(
        functools.partial(local, mesh),
        mesh=mesh,
        in_specs=(
            P(("groups", "fsdp"), None),
            P(("groups", "fsdp"), None),
            P(("groups", "fsdp")),
            P(None, "fsdp"),
            P(),
            P(),
            P(),
            P(("groups", "fsdp"), None),
        ),
        out_specs=P(("groups", "fsdp"), None),
        check_vma=False,
    )
```
